32 devices in a mesh: row: 8 (over y, x, core), col: 4 (over z).
Axes of the slice: x: 2, y: 2, z: 4, core: 2. Of those that a mesh axis runs over, the one named last changes fastest.
Arguments:
- matrix: float32 [16384, 16384], P('row', 'col'), may hold values from -9 to 9
- vectors: float32 [16384, 128], P('row'), may hold values from -0.125 to 0.125
- tfactor: float32 [128, 128], replicated, may hold values from -1 to 2, as said below
Outputs:
- updated: float32 [16384, 16384], P('row', 'col')
The draws below stay inside these ranges and needn't reach their ends.
Inputs may be any that keep to these rules, and one draw needn't show every extreme that they name: tfactor is upper triangular with its diagonal between 0.7 and 1.4.
All inputs are finite; a program needn't handle non-finite values.
Results may differ from the reference program's by a relative error of at most 0.000094.
Values sent between devices are 32-bit elements; how exact they have to be, the bound alone decides.
A program may use at most 192 MiB of HBM per device.

```python
import math
import jax
import jax.numpy as jnp
from jax import lax

M = 16384
NB = 128


def draw_matrix(key, part):
    source = jax.random.truncated_normal(key, -6.0, 6.0, (M, M), jnp.float32)
    return ((source + source.T) * 0.7071).astype(jnp.float32)


def draw_tfactor(key, part):
    first, second = jax.random.split(jax.random.fold_in(key, 7))
    diagonal = jax.random.uniform(first, (NB,), jnp.float32, 0.7, 1.4)
    upper = jax.random.truncated_normal(second, -3.0, 3.0, (NB, NB), jnp.float32) * (0.35 / math.sqrt(NB))
    return (jnp.triu(upper, 1) + jnp.diag(diagonal)).astype(jnp.float32)


def level_of(rng, extent, shards, low, high):
    factor_of = 1.0
    for dim, parts in shards:
        heights = jax.random.uniform(jax.random.fold_in(jax.random.fold_in(rng, 6), dim), (parts,), jnp.float32, low / len(shards), high / len(shards))
        factor_of = factor_of * jnp.repeat(jnp.exp(heights), extent[dim] // parts).reshape((-1,) + (1,) * (len(extent) - 1 - dim))
    return factor_of


def noise(rng, dims, deviation, reach, pieces=(), held_as=jnp.bfloat16):
    drawn = deviation * jax.random.normal(rng, dims, jnp.float32)
    if pieces:
        drawn = drawn * level_of(rng, dims, pieces, -0.22, 0.18)
    return jnp.clip(drawn, -reach, reach).astype(held_as)


def setup_inputs(seed: int = 0) -> dict:
    key_list = jax.random.split(jax.random.key(seed), 4)
    return {
        "matrix": draw_matrix(jax.random.fold_in(key_list[3], 71), 0),
        "vectors": noise(key_list[1], (M, NB), (M // 8) ** -0.5, 0.125, ((0, 8),), jnp.float32),
        "tfactor": draw_tfactor(jax.random.fold_in(key_list[3], 71), 0),
    }


def mult(left, right):
    return jnp.dot(left, right, precision=lax.Precision.HIGHEST, preferred_element_type=jnp.float32)


def reference(matrix, vectors, tfactor):
    product_x = mult(matrix, vectors)
    product_y = mult(product_x, tfactor)
    cross = mult(vectors.T, product_y)
    coupling = mult(tfactor.T, cross)
    work = product_y - 0.5 * mult(vectors, coupling)
    rows_block = math.gcd(M, 1024)
    count_blocks = M // rows_block
    tiles = matrix.reshape(count_blocks, rows_block, M)
    vec_tiles = vectors.reshape(count_blocks, rows_block, NB)
    work_tiles = work.reshape(count_blocks, rows_block, NB)

    def update(items):
        tile, vec_tile, work_tile = items
        return tile - mult(vec_tile, work.T) - mult(work_tile, vectors.T)

    result = lax.map(update, (tiles, vec_tiles, work_tiles))
    return result.reshape(M, M)
```

```python
import functools

import jax
import jax.numpy as jnp
from jax import lax
from jax.experimental import pallas as pl
from jax.experimental.pallas import tpu as pltpu
from jax.sharding import PartitionSpec as P

NT = (((1,), (1,)), ((), ()))
TN = (((0,), (0,)), ((), ()))


def product(left, right):
    return jnp.dot(left, right, precision=lax.Precision.HIGHEST, preferred_element_type=jnp.float32)


def inner_product(left, right):
    return lax.dot_general(
        left, right, TN, precision=lax.Precision.HIGHEST, preferred_element_type=jnp.float32
    )


def split(values):
    high = values.astype(jnp.bfloat16)
    low = (values - high.astype(jnp.float32)).astype(jnp.bfloat16)
    return high, low


def product_kernel(a_ref, v_ref, x_ref, v2):
    nb = v_ref.shape[1]

    @pl.when(pl.program_id(0) == 0)
    def _():
        high, low = split(v_ref[...])
        v2[:, :nb] = high
        v2[:, nb:] = low

    high, low = split(a_ref[...])
    both = jnp.dot(high, v2[...], preferred_element_type=jnp.float32)
    both += jnp.dot(low, v2[...], preferred_element_type=jnp.float32)
    x_ref[...] = both[:, :nb] + both[:, nb:]


def tile_product(matrix, vec_cols):
    rows, columns = matrix.shape
    nb = vec_cols.shape[1]
    block = min(256, rows)
    return pl.pallas_call(
        product_kernel,
        grid=(rows // block,),
        in_specs=[
            pl.BlockSpec((block, columns), lambda i: (i, 0)),
            pl.BlockSpec((columns, nb), lambda i: (0, 0)),
        ],
        out_specs=pl.BlockSpec((block, nb), lambda i: (i, 0)),
        out_shape=jax.ShapeDtypeStruct((rows, nb), jnp.float32),
        scratch_shapes=[pltpu.VMEM((columns, 2 * nb), jnp.bfloat16)],
        compiler_params=pltpu.CompilerParams(vmem_limit_bytes=56 << 20),
        name="tile_product",
    )(matrix, vec_cols)


def update_kernel(a_ref, vr_ref, wr_ref, vc_ref, wc_ref, out_ref, right):
    nb = vr_ref.shape[1]
    columns = a_ref.shape[1]
    wide = min(512, columns)

    @pl.when(pl.program_id(0) == 0)
    def _():
        for at, ref in ((0, wc_ref), (nb, vc_ref)):
            high, low = split(ref[...])
            right[:, at : at + nb] = high
            right[:, 2 * nb + at : 3 * nb + at] = low
            right[:, 4 * nb + at : 5 * nb + at] = high

    v_high, v_low = split(vr_ref[...])
    w_high, w_low = split(wr_ref[...])
    left = jnp.concatenate([v_high, w_high, v_high, w_high, v_low, w_low], axis=1)
    for at in range(0, columns, wide):
        change = lax.dot_general(
            left, right[at : at + wide, :], NT, preferred_element_type=jnp.float32
        )
        out_ref[:, at : at + wide] = a_ref[:, at : at + wide] - change


def tile_update(matrix, vectors, w_rows, vec_cols, w_cols):
    rows, columns = matrix.shape
    nb = vectors.shape[1]
    block = min(256, rows)
    return pl.pallas_call(
        update_kernel,
        grid=(rows // block,),
        in_specs=[
            pl.BlockSpec((block, columns), lambda i: (i, 0)),
            pl.BlockSpec((block, nb), lambda i: (i, 0)),
            pl.BlockSpec((block, nb), lambda i: (i, 0)),
            pl.BlockSpec((columns, nb), lambda i: (0, 0)),
            pl.BlockSpec((columns, nb), lambda i: (0, 0)),
        ],
        out_specs=pl.BlockSpec((block, columns), lambda i: (i, 0)),
        out_shape=jax.ShapeDtypeStruct((rows, columns), jnp.float32),
        scratch_shapes=[pltpu.VMEM((columns, 6 * nb), jnp.bfloat16)],
        compiler_params=pltpu.CompilerParams(vmem_limit_bytes=56 << 20),
        name="tile_update",
    )(matrix, vectors, w_rows, vec_cols, w_cols)


def to_columns(panel_rows):
    rows_here = panel_rows.shape[0]
    blocks_per = lax.axis_size("row") // lax.axis_size("col")
    gathered = lax.all_gather(panel_rows, "row", axis=0, tiled=True)
    return lax.dynamic_slice_in_dim(
        gathered, lax.axis_index("col") * (blocks_per * rows_here), blocks_per * rows_here, 0
    )


def shards(matrix, vectors, tfactor):
    vec_cols = to_columns(vectors)
    x_part = tile_product(matrix, vec_cols)
    x_rows = lax.psum(x_part, "col")
    cross = lax.psum(inner_product(vectors, x_part), ("row", "col"))
    middle = 0.5 * product(inner_product(tfactor, cross), tfactor)
    x_cols = to_columns(x_rows)
    w_rows = product(x_rows, tfactor) - product(vectors, middle)
    w_cols = product(x_cols, tfactor) - product(vec_cols, middle)
    return tile_update(matrix, vectors, w_rows, vec_cols, w_cols)


def solution(mesh):
    in_specs = (P("row", "col"), P("row", None), P())
    out_specs = P("row", "col")
    return jax.shard_map(shards, mesh=mesh, in_specs=in_specs, out_specs=out_specs, check_vma=False)
```

```python
import functools

import jax
import jax.numpy as jnp
from jax import lax
from jax.experimental import pallas as pl
from jax.experimental.pallas import tpu as pltpu
from jax.sharding import PartitionSpec as P

NN = (((1,), (0,)), ((), ()))
NT = (((1,), (1,)), ((), ()))
TN = (((0,), (0,)), ((), ()))


def split(values):
    high = values.astype(jnp.bfloat16)
    low = (values - high.astype(jnp.float32)).astype(jnp.bfloat16)
    return high, low


def wide_dot(left, right, dims):
    l_high, l_low = split(left)
    r_high, r_low = split(right)
    return (
        lax.dot_general(l_high, r_high, dims, preferred_element_type=jnp.float32)
        + lax.dot_general(l_high, r_low, dims, preferred_element_type=jnp.float32)
        + lax.dot_general(l_low, r_high, dims, preferred_element_type=jnp.float32)
    )


CHUNKS = 8
LAG = 2
MESH = pl.DeviceIdType.MESH


def remote(src, dst, send_sem, recv_sem, device):
    return pltpu.make_async_remote_copy(
        src_ref=src, dst_ref=dst, send_sem=send_sem, recv_sem=recv_sem,
        device_id=device, device_id_type=MESH,
    )


def panel_kernel(
    row_count, col_count, a_hbm, v_ref, vc_out, xr_out, xc_out, g_out,
    a, vc, v2, part, rs_in, xr, xc, g_sum, g_in,
    a_sem, out_sem, v_ring_s, v_ring_r, v_sib_s, v_sib_r, x_ring_s, x_ring_r, x_sib_s, x_sib_r,
    rs_s, rs_r, ag_s, ag_r, g_s, g_r,
):
    m, nb = v_ref.shape
    half = m // 2
    chunk = half // CHUNKS
    chips = row_count // 2
    sources = chips // col_count
    last = col_count - 1
    wide = 1
    while wide * wide < chips:
        wide *= 2

    row, col = lax.axis_index("row"), lax.axis_index("col")
    chip, core = row // 2, row % 2

    def snake(at):
        y, x = at // wide, at % wide
        return y * wide + x + (y % 2) * (wide - 1 - 2 * x)

    place = snake(chip)
    sibling = (row + 1 - 2 * core, col)
    onward = (snake((place + 1) % chips) * 2 + core, col)
    backward = (snake((place + chips - 1) % chips) * 2 + core, col)
    ring = (onward, backward)
    right, left = (row, (col + 1) % col_count), (row, (col + last) % col_count)
    pairs = []
    bit = 1
    while bit < row_count:
        pairs.append((row + (1 - 2 * ((row // bit) % 2)) * bit, col))
        bit *= 2
    bit = 1
    while bit < col_count:
        pairs.append((row, col + (1 - 2 * ((col // bit) % 2)) * bit))
        bit *= 2

    def slab(h, i):
        return pl.ds(pl.multiple_of(h * half + i * chunk, chunk), chunk)

    def load(h, i):
        return pltpu.make_async_copy(a_hbm.at[slab(h, i)], a.at[slab(h, i)], a_sem.at[h, i])

    @pl.loop(0, CHUNKS)
    def _(i):
        load(0, i).start()
        load(1, i).start()

    barrier = pltpu.get_barrier_semaphore()
    greeted = [sibling, onward, backward, right, left] + pairs
    for device in greeted:
        pl.semaphore_signal(barrier, inc=1, device_id=device, device_id_type=MESH)
    pl.semaphore_wait(barrier, len(greeted))

    def distances(s):
        start = snake(col * sources + s)
        return (place - start + chips) % chips, (start - place + chips) % chips

    def block(s, whose, h, i):
        return pl.ds(pl.multiple_of((2 * s + whose) * m + h * half + i * chunk, chunk), chunk)

    def ring_copy(buf, sems, s, h, i):
        at = buf.at[block(s, core, h, i)]
        return remote(at, at, sems[0].at[s, h, i], sems[1].at[s, h, i], ring[h])

    def sib_copy(buf, sems, s, h, i, whose):
        at = buf.at[block(s, whose, h, i)]
        return remote(at, at, sems[2].at[s, h, i], sems[3].at[s, h, i], sibling)

    def spread(buf, sems, s, h, step):
        away = distances(s)[h]
        i = step - LAG * away
        live = (i >= 0) & (i < CHUNKS)

        @pl.when(live & (away > 0))
        def _():
            ring_copy(buf, sems, s, h, i).wait_recv()

        @pl.when(live & (away < chips - 1))
        def _():
            ring_copy(buf, sems, s, h, i).start()

        @pl.when(live)
        def _():
            sib_copy(buf, sems, s, h, i, core).start()

    def spread_sent(buf, sems, s, h, i):
        @pl.when(distances(s)[h] < chips - 1)
        def _():
            ring_copy(buf, sems, s, h, i).wait_send()

        sib_copy(buf, sems, s, h, i, core).wait_send()

    v_sems = (v_ring_s, v_ring_r, v_sib_s, v_sib_r)
    x_sems = (x_ring_s, x_ring_r, x_sib_s, x_sib_r)

    for s in range(sources):
        @pl.when(chip == col * sources + s)
        def _():
            vc[pl.ds(pl.multiple_of((2 * s + core) * m, m), m), :] = v_ref[...]

    @pl.loop(0, CHUNKS + LAG * (chips - 1))
    def _(t):
        for s in range(sources):
            for h in range(2):
                spread(vc, v_sems, s, h, t)

    @pl.loop(0, CHUNKS)
    def _(i):
        for s in range(sources):
            for h in range(2):
                sib_copy(vc, v_sems, s, h, i, 1 - core).wait_recv()

    vc_copy = pltpu.make_async_copy(vc, vc_out, out_sem.at[0])
    vc_copy.start()

    v_high, v_low = split(vc[...])
    v2[:, :nb] = v_high
    v2[:, nb:] = v_low
    g_sum[0] = jnp.zeros((nb, nb), jnp.float32)

    def rs_copy(h, i):
        return remote(
            part.at[slab(h, i)], rs_in.at[slab(h, i)], rs_s.at[h, i], rs_r.at[h, i], (left, right)[h]
        )

    def ag_copy(h, i):
        at = xr.at[slab(h, i)]
        return remote(at, at, ag_s.at[h, i], ag_r.at[h, i], (right, left)[h])

    def g_copy(j):
        return remote(g_sum.at[j], g_in.at[j], g_s.at[j], g_r.at[j], pairs[j])

    @pl.loop(0, CHUNKS + LAG * (2 * last + chips - 1))
    def _(t):
        @pl.when(t < CHUNKS)
        def _():
            load(0, t).wait()
            load(1, t).wait()
            parts = split(a[slab(0, t), :]) + split(a[slab(1, t), :])
            both = jnp.dot(jnp.concatenate(parts, axis=0), v2[...], preferred_element_type=jnp.float32)
            both = both[:, :nb] + both[:, nb:]
            first = both[:chunk] + both[chunk : 2 * chunk]
            second = both[2 * chunk : 3 * chunk] + both[3 * chunk :]
            part[slab(0, t), :] = first
            part[slab(1, t), :] = second
            g_sum[0] += wide_dot(v_ref[slab(0, t), :], first, TN) + wide_dot(
                v_ref[slab(1, t), :], second, TN
            )

        for h in range(2):
            depth = last - col if h == 0 else col
            i = t - LAG * depth
            live = (i >= 0) & (i < CHUNKS)

            @pl.when(live & (depth > 0))
            def _():
                rs_copy(h, i).wait_recv()
                part[slab(h, i), :] += rs_in[slab(h, i), :]

            @pl.when(live & (depth < last))
            def _():
                rs_copy(h, i).start()

            @pl.when(live & (depth == last))
            def _():
                xr[slab(h, i), :] = part[slab(h, i), :]

        for h in range(2):
            far = col if h == 0 else last - col
            i = t - LAG * (last + far)
            live = (i >= 0) & (i < CHUNKS)

            @pl.when(live & (far > 0))
            def _():
                ag_copy(h, i).wait_recv()

            @pl.when(live & (far < last))
            def _():
                ag_copy(h, i).start()

            for s in range(sources):
                @pl.when(live & (chip == col * sources + s))
                def _():
                    xc[block(s, core, h, i), :] = xr[slab(h, i), :]

                spread(xc, x_sems, s, h, t - LAG * (last + far))

        for j in range(len(pairs) + 1):
            @pl.when(t == CHUNKS - 1 + LAG * j)
            def _():
                if j > 0:
                    g_copy(j - 1).wait_recv()
                    g_sum[j] = g_sum[j - 1] + g_in[j - 1]
                if j < len(pairs):
                    g_copy(j).start()

    xr_copy = pltpu.make_async_copy(xr, xr_out, out_sem.at[1])
    xr_copy.start()
    g_out[...] = g_sum[len(pairs)]

    @pl.loop(0, CHUNKS)
    def _(i):
        for s in range(sources):
            for h in range(2):
                sib_copy(xc, x_sems, s, h, i, 1 - core).wait_recv()

    xc_copy = pltpu.make_async_copy(xc, xc_out, out_sem.at[2])
    xc_copy.start()

    @pl.loop(0, CHUNKS)
    def _(i):
        for s in range(sources):
            for h in range(2):
                spread_sent(vc, v_sems, s, h, i)
                spread_sent(xc, x_sems, s, h, i)
        for h in range(2):
            depth = last - col if h == 0 else col

            @pl.when(depth < last)
            def _():
                rs_copy(h, i).wait_send()

            far = col if h == 0 else last - col

            @pl.when(far < last)
            def _():
                ag_copy(h, i).wait_send()

    for j in range(len(pairs)):
        g_copy(j).wait_send()
    vc_copy.wait()
    xr_copy.wait()
    xc_copy.wait()


def panel(matrix, vectors):
    m, n = matrix.shape
    nb = vectors.shape[1]
    rows, cols = lax.axis_size("row"), lax.axis_size("col")
    sources = rows // 2 // cols
    steps = (rows - 1).bit_length() + (cols - 1).bit_length()
    f32 = jnp.float32
    dma = pltpu.SemaphoreType.DMA
    whole = pl.BlockSpec(memory_space=pltpu.VMEM)
    hbm = pl.BlockSpec(memory_space=pl.ANY)
    return pl.pallas_call(
        functools.partial(panel_kernel, rows, cols),
        in_specs=[hbm, whole],
        out_specs=[hbm, hbm, hbm, whole],
        out_shape=[
            jax.ShapeDtypeStruct((n, nb), f32),
            jax.ShapeDtypeStruct((m, nb), f32),
            jax.ShapeDtypeStruct((n, nb), f32),
            jax.ShapeDtypeStruct((nb, nb), f32),
        ],
        scratch_shapes=[
            pltpu.VMEM((m, n), f32),
            pltpu.VMEM((n, nb), f32),
            pltpu.VMEM((n, 2 * nb), jnp.bfloat16),
            pltpu.VMEM((m, nb), f32),
            pltpu.VMEM((m, nb), f32),
            pltpu.VMEM((m, nb), f32),
            pltpu.VMEM((n, nb), f32),
            pltpu.VMEM((steps + 1, nb, nb), f32),
            pltpu.VMEM((steps, nb, nb), f32),
            dma((2, CHUNKS)),
            dma((3,)),
        ]
        + [dma((sources, 2, CHUNKS))] * 8
        + [dma((2, CHUNKS))] * 4
        + [dma((steps,))] * 2,
        compiler_params=pltpu.CompilerParams(
            collective_id=0, has_side_effects=True, vmem_limit_bytes=60 << 20
        ),
        name="panel_products",
    )(matrix, vectors)


def update_kernel(a_ref, v_ref, xr_ref, t_ref, g_ref, vc_ref, xc_ref, out_ref, right, middle):
    nb = v_ref.shape[1]
    columns = a_ref.shape[1]
    wide = min(512, columns)

    @pl.when(pl.program_id(0) == 0)
    def _():
        half = 0.5 * wide_dot(wide_dot(t_ref[...], g_ref[...], TN), t_ref[...], NN)
        middle[...] = half + half.T
        for at, ref in ((0, xc_ref), (nb, vc_ref)):
            high, low = split(ref[...])
            right[:, at : at + nb] = high
            right[:, 2 * nb + at : 3 * nb + at] = low
            right[:, 4 * nb + at : 5 * nb + at] = high

    vectors = v_ref[...]
    l_high, l_low = split(wide_dot(vectors, t_ref[...], NT))
    w_high, w_low = split(
        wide_dot(xr_ref[...], t_ref[...], NN) - wide_dot(vectors, middle[...], NN)
    )
    left = jnp.concatenate([l_high, w_high, l_high, w_high, l_low, w_low], axis=1)
    for at in range(0, columns, wide):
        change = lax.dot_general(
            left, right[at : at + wide, :], NT, preferred_element_type=jnp.float32
        )
        out_ref[:, at : at + wide] = a_ref[:, at : at + wide] - change


def tile_update(matrix, vectors, x_rows, tfactor, cross, vec_cols, x_cols):
    rows, columns = matrix.shape
    nb = vectors.shape[1]
    block = min(256, rows)
    panel_rows = pl.BlockSpec((block, nb), lambda i: (i, 0))
    small = pl.BlockSpec((nb, nb), lambda i: (0, 0))
    panel_cols = pl.BlockSpec((columns, nb), lambda i: (0, 0))
    tile = pl.BlockSpec((block, columns), lambda i: (i, 0))
    return pl.pallas_call(
        update_kernel,
        grid=(rows // block,),
        in_specs=[tile, panel_rows, panel_rows, small, small, panel_cols, panel_cols],
        out_specs=tile,
        out_shape=jax.ShapeDtypeStruct((rows, columns), jnp.float32),
        scratch_shapes=[
            pltpu.VMEM((columns, 6 * nb), jnp.bfloat16),
            pltpu.VMEM((nb, nb), jnp.float32),
        ],
        compiler_params=pltpu.CompilerParams(vmem_limit_bytes=56 << 20),
        name="tile_update",
    )(matrix, vectors, x_rows, tfactor, cross, vec_cols, x_cols)


def shards(matrix, vectors, tfactor):
    vec_cols, x_rows, x_cols, cross = panel(matrix, vectors)
    return tile_update(matrix, vectors, x_rows, tfactor, cross, vec_cols, x_cols)


def solution(mesh):
    in_specs = (P("row", "col"), P("row", None), P())
    out_specs = P("row", "col")
    return jax.shard_map(shards, mesh=mesh, in_specs=in_specs, out_specs=out_specs, check_vma=False)
```

```python
import functools

import jax
import jax.numpy as jnp
from jax import lax
from jax.experimental import pallas as pl
from jax.experimental.pallas import tpu as pltpu
from jax.sharding import PartitionSpec as P

NN = (((1,), (0,)), ((), ()))
NT = (((1,), (1,)), ((), ()))
TN = (((0,), (0,)), ((), ()))


def split(values):
    high = values.astype(jnp.bfloat16)
    low = (values - high.astype(jnp.float32)).astype(jnp.bfloat16)
    return high, low


def wide_dot(left, right, dims):
    l_high, l_low = split(left)
    r_high, r_low = split(right)
    return (
        lax.dot_general(l_high, r_high, dims, preferred_element_type=jnp.float32)
        + lax.dot_general(l_high, r_low, dims, preferred_element_type=jnp.float32)
        + lax.dot_general(l_low, r_high, dims, preferred_element_type=jnp.float32)
    )


CHUNKS = 16
LAG = 2
SLOTS = 4
MESH = pl.DeviceIdType.MESH


def remote(src, dst, send_sem, recv_sem, device):
    return pltpu.make_async_remote_copy(
        src_ref=src, dst_ref=dst, send_sem=send_sem, recv_sem=recv_sem,
        device_id=device, device_id_type=MESH,
    )


def panel_kernel(
    row_count, col_count, a_hbm, v_ref, right_out, xr_out, g_out,
    a, a2, right_t, vc, v2, part, rs_in, xr, xc, g_sum, g_in,
    a_sem, out_sem, v_ring_s, v_ring_r, v_sib_s, v_sib_r, x_ring_s, x_ring_r, x_sib_s, x_sib_r,
    rs_s, rs_r, ag_s, ag_r, g_s, g_r,
):
    m, nb = v_ref.shape
    half = m // 2
    chunk = half // CHUNKS
    chips = row_count // 2
    sources = chips // col_count
    last = col_count - 1
    wide = 1
    while wide * wide < chips:
        wide *= 2

    row, col = lax.axis_index("row"), lax.axis_index("col")
    chip, core = row // 2, row % 2

    def snake(at):
        y, x = at // wide, at % wide
        return y * wide + x + (y % 2) * (wide - 1 - 2 * x)

    place = snake(chip)
    sibling = (row + 1 - 2 * core, col)
    onward = (snake((place + 1) % chips) * 2 + core, col)
    backward = (snake((place + chips - 1) % chips) * 2 + core, col)
    ring = (onward, backward)
    right, left = (row, (col + 1) % col_count), (row, (col + last) % col_count)
    pairs = []
    bit = 1
    while bit < row_count:
        pairs.append((row + (1 - 2 * ((row // bit) % 2)) * bit, col))
        bit *= 2
    bit = 1
    while bit < col_count:
        pairs.append((row, col + (1 - 2 * ((col // bit) % 2)) * bit))
        bit *= 2

    def slab(h, i):
        return pl.ds(pl.multiple_of(h * half + i * chunk, chunk), chunk)

    def load(h, i):
        slot = i % SLOTS
        return pltpu.make_async_copy(a_hbm.at[slab(h, i)], a.at[slot, h], a_sem.at[slot, h])

    for i in range(SLOTS):
        load(0, i).start()
        load(1, i).start()

    barrier = pltpu.get_barrier_semaphore()
    greeted = [sibling, onward, backward, right, left] + pairs
    for device in greeted:
        pl.semaphore_signal(barrier, inc=1, device_id=device, device_id_type=MESH)
    pl.semaphore_wait(barrier, len(greeted))

    def distances(s):
        start = snake(col * sources + s)
        return (place - start + chips) % chips, (start - place + chips) % chips

    def block(s, whose, h, i):
        return pl.ds(pl.multiple_of((2 * s + whose) * m + h * half + i * chunk, chunk), chunk)

    def ring_copy(buf, sems, s, h, i):
        at = buf.at[block(s, core, h, i)]
        return remote(at, at, sems[0].at[s, h, i], sems[1].at[s, h, i], ring[h])

    def sib_copy(buf, sems, s, h, i, whose):
        at = buf.at[block(s, whose, h, i)]
        return remote(at, at, sems[2].at[s, h, i], sems[3].at[s, h, i], sibling)

    def spread(buf, sems, s, h, step):
        away = distances(s)[h]
        i = step - LAG * away
        live = (i >= 0) & (i < CHUNKS)

        @pl.when(live & (away > 0))
        def _():
            ring_copy(buf, sems, s, h, i).wait_recv()

        @pl.when(live & (away < chips - 1))
        def _():
            ring_copy(buf, sems, s, h, i).start()

        @pl.when(live)
        def _():
            sib_copy(buf, sems, s, h, i, core).start()

    def spread_sent(buf, sems, s, h, i):
        @pl.when(distances(s)[h] < chips - 1)
        def _():
            ring_copy(buf, sems, s, h, i).wait_send()

        sib_copy(buf, sems, s, h, i, core).wait_send()

    v_sems = (v_ring_s, v_ring_r, v_sib_s, v_sib_r)
    x_sems = (x_ring_s, x_ring_r, x_sib_s, x_sib_r)

    for s in range(sources):
        @pl.when(chip == col * sources + s)
        def _():
            vc[pl.ds(pl.multiple_of((2 * s + core) * m, m), m), :] = v_ref[...]

    @pl.loop(0, CHUNKS + LAG * (chips - 1))
    def _(t):
        for s in range(sources):
            for h in range(2):
                spread(vc, v_sems, s, h, t)

        @pl.when(t < CHUNKS)
        def _():
            for h in range(2):
                load(h, t).wait()
                high, low = split(a[t % SLOTS, h])
                a2[pl.ds(pl.multiple_of((4 * t + 2 * h) * chunk, chunk), chunk), :] = high
                a2[pl.ds(pl.multiple_of((4 * t + 2 * h + 1) * chunk, chunk), chunk), :] = low

        @pl.when(t + SLOTS < CHUNKS)
        def _():
            load(0, t + SLOTS).start()
            load(1, t + SLOTS).start()

    @pl.loop(0, CHUNKS)
    def _(i):
        for s in range(sources):
            for h in range(2):
                sib_copy(vc, v_sems, s, h, i, 1 - core).wait_recv()

    tile = min(512, vc.shape[0])
    tiles = vc.shape[0] // tile

    def turn(source, at, j):
        here = pl.ds(pl.multiple_of(j * tile, tile), tile)
        high, low = split(source[here, :].T)
        right_t[at : at + nb, here] = high
        right_t[2 * nb + at : 3 * nb + at, here] = low

    v_high, v_low = split(vc[...])
    v2[:, :nb] = v_high
    v2[:, nb:] = v_low
    g_sum[0] = jnp.zeros((nb, nb), jnp.float32)

    def rs_copy(h, i):
        return remote(
            part.at[slab(h, i)], rs_in.at[slab(h, i)], rs_s.at[h, i], rs_r.at[h, i], (left, right)[h]
        )

    def ag_copy(h, i):
        at = xr.at[slab(h, i)]
        return remote(at, at, ag_s.at[h, i], ag_r.at[h, i], (right, left)[h])

    def g_copy(j):
        return remote(g_sum.at[j], g_in.at[j], g_s.at[j], g_r.at[j], pairs[j])

    @pl.loop(0, CHUNKS + LAG * (2 * last + chips - 1))
    def _(t):
        @pl.when(t < CHUNKS)
        def _():
            parts = a2[pl.ds(pl.multiple_of(4 * t * chunk, 4 * chunk), 4 * chunk), :]
            both = jnp.dot(parts, v2[...], preferred_element_type=jnp.float32)
            both = both[:, :nb] + both[:, nb:]
            first = both[:chunk] + both[chunk : 2 * chunk]
            second = both[2 * chunk : 3 * chunk] + both[3 * chunk :]
            part[slab(0, t), :] = first
            part[slab(1, t), :] = second
            g_sum[0] += wide_dot(v_ref[slab(0, t), :], first, TN) + wide_dot(
                v_ref[slab(1, t), :], second, TN
            )

        for h in range(2):
            depth = last - col if h == 0 else col
            i = t - LAG * depth
            live = (i >= 0) & (i < CHUNKS)

            @pl.when(live & (depth > 0))
            def _():
                rs_copy(h, i).wait_recv()
                part[slab(h, i), :] += rs_in[slab(h, i), :]

            @pl.when(live & (depth < last))
            def _():
                rs_copy(h, i).start()

            @pl.when(live & (depth == last))
            def _():
                xr[slab(h, i), :] = part[slab(h, i), :]

        for h in range(2):
            far = col if h == 0 else last - col
            i = t - LAG * (last + far)
            live = (i >= 0) & (i < CHUNKS)

            @pl.when(live & (far > 0))
            def _():
                ag_copy(h, i).wait_recv()

            @pl.when(live & (far < last))
            def _():
                ag_copy(h, i).start()

            for s in range(sources):
                @pl.when(live & (chip == col * sources + s))
                def _():
                    xc[block(s, core, h, i), :] = xr[slab(h, i), :]

                spread(xc, x_sems, s, h, t - LAG * (last + far))

        @pl.when((t >= CHUNKS) & (t < CHUNKS + tiles))
        def _():
            turn(vc, nb, t - CHUNKS)

        for j in range(len(pairs) + 1):
            @pl.when(t == CHUNKS - 1 + LAG * j)
            def _():
                if j > 0:
                    g_copy(j - 1).wait_recv()
                    g_sum[j] = g_sum[j - 1] + g_in[j - 1]
                if j < len(pairs):
                    g_copy(j).start()

    xr_copy = pltpu.make_async_copy(xr, xr_out, out_sem.at[1])
    xr_copy.start()
    g_out[...] = g_sum[len(pairs)]

    @pl.loop(0, CHUNKS)
    def _(i):
        for s in range(sources):
            for h in range(2):
                sib_copy(xc, x_sems, s, h, i, 1 - core).wait_recv()

    @pl.loop(0, tiles)
    def _(j):
        turn(xc, 0, j)

    right_copy = pltpu.make_async_copy(right_t, right_out, out_sem.at[0])
    right_copy.start()

    @pl.loop(0, CHUNKS)
    def _(i):
        for s in range(sources):
            for h in range(2):
                spread_sent(vc, v_sems, s, h, i)
                spread_sent(xc, x_sems, s, h, i)
        for h in range(2):
            depth = last - col if h == 0 else col

            @pl.when(depth < last)
            def _():
                rs_copy(h, i).wait_send()

            far = col if h == 0 else last - col

            @pl.when(far < last)
            def _():
                ag_copy(h, i).wait_send()

    for j in range(len(pairs)):
        g_copy(j).wait_send()
    right_copy.wait()
    xr_copy.wait()


def panel(matrix, vectors):
    m, n = matrix.shape
    nb = vectors.shape[1]
    rows, cols = lax.axis_size("row"), lax.axis_size("col")
    sources = rows // 2 // cols
    steps = (rows - 1).bit_length() + (cols - 1).bit_length()
    f32 = jnp.float32
    dma = pltpu.SemaphoreType.DMA
    whole = pl.BlockSpec(memory_space=pltpu.VMEM)
    hbm = pl.BlockSpec(memory_space=pl.ANY)
    return pl.pallas_call(
        functools.partial(panel_kernel, rows, cols),
        in_specs=[hbm, whole],
        out_specs=[hbm, hbm, whole],
        out_shape=[
            jax.ShapeDtypeStruct((4 * nb, n), jnp.bfloat16),
            jax.ShapeDtypeStruct((m, nb), f32),
            jax.ShapeDtypeStruct((nb, nb), f32),
        ],
        scratch_shapes=[
            pltpu.VMEM((SLOTS, 2, m // 2 // CHUNKS, n), f32),
            pltpu.VMEM((2 * m, n), jnp.bfloat16),
            pltpu.VMEM((4 * nb, n), jnp.bfloat16),
            pltpu.VMEM((n, nb), f32),
            pltpu.VMEM((n, 2 * nb), jnp.bfloat16),
            pltpu.VMEM((m, nb), f32),
            pltpu.VMEM((m, nb), f32),
            pltpu.VMEM((m, nb), f32),
            pltpu.VMEM((n, nb), f32),
            pltpu.VMEM((steps + 1, nb, nb), f32),
            pltpu.VMEM((steps, nb, nb), f32),
            dma((SLOTS, 2)),
            dma((2,)),
        ]
        + [dma((sources, 2, CHUNKS))] * 8
        + [dma((2, CHUNKS))] * 4
        + [dma((steps,))] * 2,
        compiler_params=pltpu.CompilerParams(
            collective_id=0, has_side_effects=True, vmem_limit_bytes=62 << 20
        ),
        name="panel_products",
    )(matrix, vectors)


def update_kernel(a_ref, v_ref, xr_ref, t_ref, g_ref, right_ref, out_ref, middle):
    nb = v_ref.shape[1]
    columns = a_ref.shape[1]
    wide = min(512, columns)

    @pl.when(pl.program_id(0) == 0)
    def _():
        half = 0.5 * wide_dot(wide_dot(t_ref[...], g_ref[...], TN), t_ref[...], NN)
        middle[...] = half + half.T

    vectors = v_ref[...]
    l_high, l_low = split(wide_dot(vectors, t_ref[...], NT))
    w_high, w_low = split(
        wide_dot(xr_ref[...], t_ref[...], NN) - wide_dot(vectors, middle[...], NN)
    )
    left = jnp.concatenate([l_high, w_high, l_high, w_high, l_low, w_low], axis=1)
    for at in range(0, columns, wide):
        high = right_ref[: 2 * nb, at : at + wide]
        low = right_ref[2 * nb :, at : at + wide]
        change = jnp.dot(
            left, jnp.concatenate([high, low, high], axis=0), preferred_element_type=jnp.float32
        )
        out_ref[:, at : at + wide] = a_ref[:, at : at + wide] - change


def tile_update(matrix, vectors, x_rows, tfactor, cross, right):
    rows, columns = matrix.shape
    nb = vectors.shape[1]
    block = min(256, rows)
    panel_rows = pl.BlockSpec((block, nb), lambda i: (i, 0))
    small = pl.BlockSpec((nb, nb), lambda i: (0, 0))
    tile = pl.BlockSpec((block, columns), lambda i: (i, 0))
    return pl.pallas_call(
        update_kernel,
        grid=(rows // block,),
        in_specs=[
            tile, panel_rows, panel_rows, small, small,
            pl.BlockSpec((4 * nb, columns), lambda i: (0, 0)),
        ],
        out_specs=tile,
        out_shape=jax.ShapeDtypeStruct((rows, columns), jnp.float32),
        scratch_shapes=[pltpu.VMEM((nb, nb), jnp.float32)],
        compiler_params=pltpu.CompilerParams(vmem_limit_bytes=56 << 20),
        name="tile_update",
    )(matrix, vectors, x_rows, tfactor, cross, right)


def shards(matrix, vectors, tfactor):
    right, x_rows, cross = panel(matrix, vectors)
    return tile_update(matrix, vectors, x_rows, tfactor, cross, right)


def solution(mesh):
    in_specs = (P("row", "col"), P("row", None), P())
    out_specs = P("row", "col")
    return jax.shard_map(shards, mesh=mesh, in_specs=in_specs, out_specs=out_specs, check_vma=False)
```

```python
import functools

import jax
import jax.numpy as jnp
from jax import lax
from jax.experimental import pallas as pl
from jax.experimental.pallas import tpu as pltpu
from jax.sharding import PartitionSpec as P

NN = (((1,), (0,)), ((), ()))
NT = (((1,), (1,)), ((), ()))
TN = (((0,), (0,)), ((), ()))


def split(values):
    high = values.astype(jnp.bfloat16)
    low = (values - high.astype(jnp.float32)).astype(jnp.bfloat16)
    return high, low


def wide_dot(left, right, dims):
    l_high, l_low = split(left)
    r_high, r_low = split(right)
    return (
        lax.dot_general(l_high, r_high, dims, preferred_element_type=jnp.float32)
        + lax.dot_general(l_high, r_low, dims, preferred_element_type=jnp.float32)
        + lax.dot_general(l_low, r_high, dims, preferred_element_type=jnp.float32)
    )


CHUNKS = 8
LAG = 2
SLOTS = 3
KEPT = 4
MESH = pl.DeviceIdType.MESH


def remote(src, dst, send_sem, recv_sem, device):
    return pltpu.make_async_remote_copy(
        src_ref=src, dst_ref=dst, send_sem=send_sem, recv_sem=recv_sem,
        device_id=device, device_id_type=MESH,
    )


def panel_kernel(
    row_count, col_count, a_hbm, v_ref, keep_out, right_out, xr_out, g_out,
    a, right_t, vc, v2, part, rs_in, xr, xc, g_sum, g_in,
    a_sem, keep_sem, out_sem, v_ring_s, v_ring_r, v_sib_s, v_sib_r, x_ring_s, x_ring_r, x_sib_s, x_sib_r,
    rs_s, rs_r, ag_s, ag_r, g_s, g_r,
):
    m, nb = v_ref.shape
    half = m // 2
    chunk = half // CHUNKS
    chips = row_count // 2
    sources = chips // col_count
    last = col_count - 1
    wide = 1
    while wide * wide < chips:
        wide *= 2

    row, col = lax.axis_index("row"), lax.axis_index("col")
    chip, core = row // 2, row % 2

    def snake(at):
        y, x = at // wide, at % wide
        return y * wide + x + (y % 2) * (wide - 1 - 2 * x)

    place = snake(chip)
    sibling = (row + 1 - 2 * core, col)
    onward = (snake((place + 1) % chips) * 2 + core, col)
    backward = (snake((place + chips - 1) % chips) * 2 + core, col)
    ring = (onward, backward)
    right, left = (row, (col + 1) % col_count), (row, (col + last) % col_count)
    pairs = []
    bit = 1
    while bit < row_count:
        pairs.append((row + (1 - 2 * ((row // bit) % 2)) * bit, col))
        bit *= 2
    bit = 1
    while bit < col_count:
        pairs.append((row, col + (1 - 2 * ((col // bit) % 2)) * bit))
        bit *= 2

    def slab(h, i):
        return pl.ds(pl.multiple_of(h * half + i * chunk, chunk), chunk)

    def load(u):
        slot = u % SLOTS
        return pltpu.make_async_copy(a_hbm.at[slab(u % 2, u // 2)], a.at[slot], a_sem.at[slot])

    def keep(i):
        at = pl.ds(pl.multiple_of(2 * i * chunk, 2 * chunk), 2 * chunk)
        return pltpu.make_async_copy(a_hbm.at[at], keep_out.at[at], keep_sem.at[i])

    for u in range(SLOTS):
        load(u).start()
    for i in range(KEPT):
        keep(i).start()

    barrier = pltpu.get_barrier_semaphore()
    greeted = [sibling, onward, backward, right, left] + pairs
    for device in greeted:
        pl.semaphore_signal(barrier, inc=1, device_id=device, device_id_type=MESH)
    pl.semaphore_wait(barrier, len(greeted))

    def distances(s):
        start = snake(col * sources + s)
        return (place - start + chips) % chips, (start - place + chips) % chips

    def block(s, whose, h, i):
        return pl.ds(pl.multiple_of((2 * s + whose) * m + h * half + i * chunk, chunk), chunk)

    def ring_copy(buf, sems, s, h, i):
        at = buf.at[block(s, core, h, i)]
        return remote(at, at, sems[0].at[s, h, i], sems[1].at[s, h, i], ring[h])

    def sib_copy(buf, sems, s, h, i, whose):
        at = buf.at[block(s, whose, h, i)]
        return remote(at, at, sems[2].at[s, h, i], sems[3].at[s, h, i], sibling)

    def spread(buf, sems, s, h, step):
        away = distances(s)[h]
        i = step - LAG * away
        live = (i >= 0) & (i < CHUNKS)

        @pl.when(live & (away > 0))
        def _():
            ring_copy(buf, sems, s, h, i).wait_recv()

        @pl.when(live & (away < chips - 1))
        def _():
            ring_copy(buf, sems, s, h, i).start()

        @pl.when(live)
        def _():
            sib_copy(buf, sems, s, h, i, core).start()

    def spread_sent(buf, sems, s, h, i):
        @pl.when(distances(s)[h] < chips - 1)
        def _():
            ring_copy(buf, sems, s, h, i).wait_send()

        sib_copy(buf, sems, s, h, i, core).wait_send()

    v_sems = (v_ring_s, v_ring_r, v_sib_s, v_sib_r)
    x_sems = (x_ring_s, x_ring_r, x_sib_s, x_sib_r)

    for s in range(sources):
        @pl.when(chip == col * sources + s)
        def _():
            vc[pl.ds(pl.multiple_of((2 * s + core) * m, m), m), :] = v_ref[...]

    @pl.loop(0, CHUNKS + LAG * (chips - 1))
    def _(t):
        for s in range(sources):
            for h in range(2):
                spread(vc, v_sems, s, h, t)

    @pl.loop(0, CHUNKS)
    def _(i):
        for s in range(sources):
            for h in range(2):
                sib_copy(vc, v_sems, s, h, i, 1 - core).wait_recv()

    tile = min(512, vc.shape[0])
    tiles = vc.shape[0] // tile

    def turn(source, at, j):
        here = pl.ds(pl.multiple_of(j * tile, tile), tile)
        high, low = split(source[here, :].T)
        right_t[at : at + nb, here] = high
        right_t[2 * nb + at : 3 * nb + at, here] = low

    v_high, v_low = split(vc[...])
    v2[:, :nb] = v_high
    v2[:, nb:] = v_low
    g_sum[0] = jnp.zeros((nb, nb), jnp.float32)

    def rs_copy(h, i):
        return remote(
            part.at[slab(h, i)], rs_in.at[slab(h, i)], rs_s.at[h, i], rs_r.at[h, i], (left, right)[h]
        )

    def ag_copy(h, i):
        at = xr.at[slab(h, i)]
        return remote(at, at, ag_s.at[h, i], ag_r.at[h, i], (right, left)[h])

    def g_copy(j):
        return remote(g_sum.at[j], g_in.at[j], g_s.at[j], g_r.at[j], pairs[j])

    @pl.loop(0, CHUNKS + LAG * (2 * last + chips - 1))
    def _(t):
        @pl.when(t < CHUNKS)
        def _():
            for h in range(2):
                u = 2 * t + h
                load(u).wait()
                pieces = jnp.concatenate(split(a[u % SLOTS]), axis=0)
                both = jnp.dot(pieces, v2[...], preferred_element_type=jnp.float32)
                both = both[:chunk] + both[chunk:]
                both = both[:, :nb] + both[:, nb:]
                part[slab(h, t), :] = both
                g_sum[0] += wide_dot(v_ref[slab(h, t), :], both, TN)

                @pl.when(u + SLOTS < 2 * CHUNKS)
                def _():
                    load(u + SLOTS).start()

        for h in range(2):
            depth = last - col if h == 0 else col
            i = t - LAG * depth
            live = (i >= 0) & (i < CHUNKS)

            @pl.when(live & (depth > 0))
            def _():
                rs_copy(h, i).wait_recv()
                part[slab(h, i), :] += rs_in[slab(h, i), :]

            @pl.when(live & (depth < last))
            def _():
                rs_copy(h, i).start()

            @pl.when(live & (depth == last))
            def _():
                xr[slab(h, i), :] = part[slab(h, i), :]

        for h in range(2):
            far = col if h == 0 else last - col
            i = t - LAG * (last + far)
            live = (i >= 0) & (i < CHUNKS)

            @pl.when(live & (far > 0))
            def _():
                ag_copy(h, i).wait_recv()

            @pl.when(live & (far < last))
            def _():
                ag_copy(h, i).start()

            for s in range(sources):
                @pl.when(live & (chip == col * sources + s))
                def _():
                    xc[block(s, core, h, i), :] = xr[slab(h, i), :]

                spread(xc, x_sems, s, h, t - LAG * (last + far))

        @pl.when((t >= CHUNKS) & (t < CHUNKS + tiles))
        def _():
            turn(vc, nb, t - CHUNKS)

        for j in range(len(pairs) + 1):
            @pl.when(t == CHUNKS - 1 + LAG * j)
            def _():
                if j > 0:
                    g_copy(j - 1).wait_recv()
                    g_sum[j] = g_sum[j - 1] + g_in[j - 1]
                if j < len(pairs):
                    g_copy(j).start()

    xr_copy = pltpu.make_async_copy(xr, xr_out, out_sem.at[1])
    xr_copy.start()
    g_out[...] = g_sum[len(pairs)]

    @pl.loop(0, CHUNKS)
    def _(i):
        for s in range(sources):
            for h in range(2):
                sib_copy(xc, x_sems, s, h, i, 1 - core).wait_recv()

    @pl.loop(0, tiles)
    def _(j):
        turn(xc, 0, j)

    right_copy = pltpu.make_async_copy(right_t, right_out, out_sem.at[0])
    right_copy.start()

    @pl.loop(0, CHUNKS)
    def _(i):
        for s in range(sources):
            for h in range(2):
                spread_sent(vc, v_sems, s, h, i)
                spread_sent(xc, x_sems, s, h, i)
        for h in range(2):
            depth = last - col if h == 0 else col

            @pl.when(depth < last)
            def _():
                rs_copy(h, i).wait_send()

            far = col if h == 0 else last - col

            @pl.when(far < last)
            def _():
                ag_copy(h, i).wait_send()

    for j in range(len(pairs)):
        g_copy(j).wait_send()
    for i in range(KEPT):
        keep(i).wait()
    right_copy.wait()
    xr_copy.wait()


def panel(matrix, vectors):
    m, n = matrix.shape
    nb = vectors.shape[1]
    rows, cols = lax.axis_size("row"), lax.axis_size("col")
    sources = rows // 2 // cols
    steps = (rows - 1).bit_length() + (cols - 1).bit_length()
    f32 = jnp.float32
    dma = pltpu.SemaphoreType.DMA
    whole = pl.BlockSpec(memory_space=pltpu.VMEM)
    hbm = pl.BlockSpec(memory_space=pl.ANY)
    return pl.pallas_call(
        functools.partial(panel_kernel, rows, cols),
        in_specs=[hbm, whole],
        out_specs=[hbm, hbm, hbm, whole],
        out_shape=[
            jax.ShapeDtypeStruct((m // CHUNKS * KEPT, n), f32),
            jax.ShapeDtypeStruct((4 * nb, n), jnp.bfloat16),
            jax.ShapeDtypeStruct((m, nb), f32),
            jax.ShapeDtypeStruct((nb, nb), f32),
        ],
        scratch_shapes=[
            pltpu.VMEM((SLOTS, m // 2 // CHUNKS, n), f32),
            pltpu.VMEM((4 * nb, n), jnp.bfloat16),
            pltpu.VMEM((n, nb), f32),
            pltpu.VMEM((n, 2 * nb), jnp.bfloat16),
            pltpu.VMEM((m, nb), f32),
            pltpu.VMEM((m, nb), f32),
            pltpu.VMEM((m, nb), f32),
            pltpu.VMEM((n, nb), f32),
            pltpu.VMEM((steps + 1, nb, nb), f32),
            pltpu.VMEM((steps, nb, nb), f32),
            dma((SLOTS,)),
            dma((KEPT,)),
            dma((2,)),
        ]
        + [dma((sources, 2, CHUNKS))] * 8
        + [dma((2, CHUNKS))] * 4
        + [dma((steps,))] * 2,
        compiler_params=pltpu.CompilerParams(
            collective_id=0, has_side_effects=True, vmem_limit_bytes=24 << 20
        ),
        cost_estimate=pl.CostEstimate(
            flops=8 * m * n * nb, bytes_accessed=4 * (m * n + 8 * n * nb), transcendentals=0
        ),
        name="panel_products",
    )(matrix, vectors)


def update_kernel(kept_ref, a_ref, v_ref, xr_ref, t_ref, g_ref, right_ref, out_ref, middle):
    nb = v_ref.shape[1]
    columns = a_ref.shape[1]
    wide = min(512, columns)
    from_kept = pl.program_id(0) % 2 == 0

    @pl.when(pl.program_id(0) == 0)
    def _():
        half = 0.5 * wide_dot(wide_dot(t_ref[...], g_ref[...], TN), t_ref[...], NN)
        middle[...] = half + half.T

    vectors = v_ref[...]
    l_high, l_low = split(wide_dot(vectors, t_ref[...], NT))
    w_high, w_low = split(
        wide_dot(xr_ref[...], t_ref[...], NN) - wide_dot(vectors, middle[...], NN)
    )
    left = jnp.concatenate([l_high, w_high, l_high, w_high, l_low, w_low], axis=1)
    def change(at):
        high = right_ref[: 2 * nb, at : at + wide]
        low = right_ref[2 * nb :, at : at + wide]
        return jnp.dot(
            left, jnp.concatenate([high, low, high], axis=0), preferred_element_type=jnp.float32
        )

    @pl.when(from_kept)
    def _():
        for at in range(0, columns, wide):
            out_ref[:, at : at + wide] = kept_ref[:, at : at + wide] - change(at)

    @pl.when(jnp.logical_not(from_kept))
    def _():
        for at in range(0, columns, wide):
            out_ref[:, at : at + wide] = a_ref[:, at : at + wide] - change(at)


def tile_update(kept, matrix, vectors, x_rows, tfactor, cross, right):
    rows, columns = matrix.shape
    nb = vectors.shape[1]
    block = min(128, rows)
    first = kept.shape[0] // block
    assert 2 * first * block == rows

    def here(i):
        return (i // 2 + first * (i % 2), 0)

    panel_rows = pl.BlockSpec((block, nb), here)
    small = pl.BlockSpec((nb, nb), lambda i: (0, 0))
    tile = pl.BlockSpec((block, columns), here)
    return pl.pallas_call(
        update_kernel,
        grid=(rows // block,),
        in_specs=[
            pl.BlockSpec((block, columns), lambda i: (i // 2, 0)),
            pl.BlockSpec((block, columns), lambda i: (first + i // 2, 0)),
            panel_rows, panel_rows, small, small,
            pl.BlockSpec((4 * nb, columns), lambda i: (0, 0)),
        ],
        out_specs=tile,
        out_shape=jax.ShapeDtypeStruct((rows, columns), jnp.float32),
        scratch_shapes=[pltpu.VMEM((nb, nb), jnp.float32)],
        compiler_params=pltpu.CompilerParams(vmem_limit_bytes=24 << 20),
        cost_estimate=pl.CostEstimate(
            flops=12 * rows * columns * nb, bytes_accessed=8 * rows * columns, transcendentals=0
        ),
        name="tile_update",
    )(kept, matrix, vectors, x_rows, tfactor, cross, right)


def shards(matrix, vectors, tfactor):
    kept, right, x_rows, cross = panel(matrix, vectors)
    return tile_update(kept, matrix, vectors, x_rows, tfactor, cross, right)


def solution(mesh):
    in_specs = (P("row", "col"), P("row", None), P())
    out_specs = P("row", "col")
    return jax.shard_map(shards, mesh=mesh, in_specs=in_specs, out_specs=out_specs, check_vma=False)
```

```python
import functools

import jax
import jax.numpy as jnp
from jax import lax
from jax.experimental import pallas as pl
from jax.experimental.pallas import tpu as pltpu
from jax.sharding import PartitionSpec as P

NN = (((1,), (0,)), ((), ()))
NT = (((1,), (1,)), ((), ()))
TN = (((0,), (0,)), ((), ()))


def split(values):
    high = values.astype(jnp.bfloat16)
    low = (values - high.astype(jnp.float32)).astype(jnp.bfloat16)
    return high, low


def wide_dot(left, right, dims):
    l_high, l_low = split(left)
    r_high, r_low = split(right)
    return (
        lax.dot_general(l_high, r_high, dims, preferred_element_type=jnp.float32)
        + lax.dot_general(l_high, r_low, dims, preferred_element_type=jnp.float32)
        + lax.dot_general(l_low, r_high, dims, preferred_element_type=jnp.float32)
    )


CHUNKS = 8
LAG = 2
MESH = pl.DeviceIdType.MESH


def remote(src, dst, send_sem, recv_sem, device):
    return pltpu.make_async_remote_copy(
        src_ref=src, dst_ref=dst, send_sem=send_sem, recv_sem=recv_sem,
        device_id=device, device_id_type=MESH,
    )


def panel_kernel(
    row_count, col_count, a_hbm, v_ref, vc_out, xr_out, xc_out, g_out,
    a, vc, v2, part, rs_in, xr, xc, g_sum, g_in,
    a_sem, out_sem, v_ring_s, v_ring_r, v_sib_s, v_sib_r, x_ring_s, x_ring_r, x_sib_s, x_sib_r,
    rs_s, rs_r, ag_s, ag_r, g_s, g_r,
):
    m, nb = v_ref.shape
    half = m // 2
    chunk = half // CHUNKS
    chips = row_count // 2
    sources = chips // col_count
    last = col_count - 1
    wide = 1
    while wide * wide < chips:
        wide *= 2

    row, col = lax.axis_index("row"), lax.axis_index("col")
    chip, core = row // 2, row % 2

    def snake(at):
        y, x = at // wide, at % wide
        return y * wide + x + (y % 2) * (wide - 1 - 2 * x)

    place = snake(chip)
    sibling = (row + 1 - 2 * core, col)
    onward = (snake((place + 1) % chips) * 2 + core, col)
    backward = (snake((place + chips - 1) % chips) * 2 + core, col)
    ring = (onward, backward)
    right, left = (row, (col + 1) % col_count), (row, (col + last) % col_count)
    pairs = []
    bit = 1
    while bit < row_count:
        pairs.append((row + (1 - 2 * ((row // bit) % 2)) * bit, col))
        bit *= 2
    bit = 1
    while bit < col_count:
        pairs.append((row, col + (1 - 2 * ((col // bit) % 2)) * bit))
        bit *= 2

    def slab(h, i):
        return pl.ds(pl.multiple_of(h * half + i * chunk, chunk), chunk)

    def load(h, i):
        return pltpu.make_async_copy(a_hbm.at[slab(h, i)], a.at[slab(h, i)], a_sem.at[h, i])

    @pl.loop(0, CHUNKS)
    def _(i):
        load(0, i).start()
        load(1, i).start()

    barrier = pltpu.get_barrier_semaphore()
    greeted = [sibling, onward, backward, right, left] + pairs
    for device in greeted:
        pl.semaphore_signal(barrier, inc=1, device_id=device, device_id_type=MESH)
    pl.semaphore_wait(barrier, len(greeted))

    def distances(s):
        start = snake(col * sources + s)
        return (place - start + chips) % chips, (start - place + chips) % chips

    def block(s, whose, h, i):
        return pl.ds(pl.multiple_of((2 * s + whose) * m + h * half + i * chunk, chunk), chunk)

    def ring_copy(buf, sems, s, h, i):
        at = buf.at[block(s, core, h, i)]
        return remote(at, at, sems[0].at[s, h, i], sems[1].at[s, h, i], ring[h])

    def sib_copy(buf, sems, s, h, i, whose):
        at = buf.at[block(s, whose, h, i)]
        return remote(at, at, sems[2].at[s, h, i], sems[3].at[s, h, i], sibling)

    def spread(buf, sems, s, h, step):
        away = distances(s)[h]
        i = step - LAG * away
        live = (i >= 0) & (i < CHUNKS)

        @pl.when(live & (away > 0))
        def _():
            ring_copy(buf, sems, s, h, i).wait_recv()

        @pl.when(live & (away < chips - 1))
        def _():
            ring_copy(buf, sems, s, h, i).start()

        @pl.when(live)
        def _():
            sib_copy(buf, sems, s, h, i, core).start()

    def spread_sent(buf, sems, s, h, i):
        @pl.when(distances(s)[h] < chips - 1)
        def _():
            ring_copy(buf, sems, s, h, i).wait_send()

        sib_copy(buf, sems, s, h, i, core).wait_send()

    v_sems = (v_ring_s, v_ring_r, v_sib_s, v_sib_r)
    x_sems = (x_ring_s, x_ring_r, x_sib_s, x_sib_r)

    for s in range(sources):
        @pl.when(chip == col * sources + s)
        def _():
            vc[pl.ds(pl.multiple_of((2 * s + core) * m, m), m), :] = v_ref[...]

    @pl.loop(0, CHUNKS + LAG * (chips - 1))
    def _(t):
        for s in range(sources):
            for h in range(2):
                spread(vc, v_sems, s, h, t)

    @pl.loop(0, CHUNKS)
    def _(i):
        for s in range(sources):
            for h in range(2):
                sib_copy(vc, v_sems, s, h, i, 1 - core).wait_recv()

    vc_copy = pltpu.make_async_copy(vc, vc_out, out_sem.at[0])
    vc_copy.start()

    v_high, v_low = split(vc[...])
    v2[:, :nb] = v_high
    v2[:, nb:] = v_low
    g_sum[0] = jnp.zeros((nb, nb), jnp.float32)

    def rs_copy(h, i):
        return remote(
            part.at[slab(h, i)], rs_in.at[slab(h, i)], rs_s.at[h, i], rs_r.at[h, i], (left, right)[h]
        )

    def ag_copy(h, i):
        at = xr.at[slab(h, i)]
        return remote(at, at, ag_s.at[h, i], ag_r.at[h, i], (right, left)[h])

    def g_copy(j):
        return remote(g_sum.at[j], g_in.at[j], g_s.at[j], g_r.at[j], pairs[j])

    @pl.loop(0, CHUNKS + LAG * (2 * last + chips - 1))
    def _(t):
        @pl.when(t < CHUNKS)
        def _():
            load(0, t).wait()
            load(1, t).wait()
            parts = split(a[slab(0, t), :]) + split(a[slab(1, t), :])
            both = jnp.dot(jnp.concatenate(parts, axis=0), v2[...], preferred_element_type=jnp.float32)
            both = both[:, :nb] + both[:, nb:]
            first = both[:chunk] + both[chunk : 2 * chunk]
            second = both[2 * chunk : 3 * chunk] + both[3 * chunk :]
            part[slab(0, t), :] = first
            part[slab(1, t), :] = second
            g_sum[0] += wide_dot(v_ref[slab(0, t), :], first, TN) + wide_dot(
                v_ref[slab(1, t), :], second, TN
            )

        for h in range(2):
            depth = last - col if h == 0 else col
            i = t - LAG * depth
            live = (i >= 0) & (i < CHUNKS)

            @pl.when(live & (depth > 0))
            def _():
                rs_copy(h, i).wait_recv()
                part[slab(h, i), :] += rs_in[slab(h, i), :]

            @pl.when(live & (depth < last))
            def _():
                rs_copy(h, i).start()

            @pl.when(live & (depth == last))
            def _():
                xr[slab(h, i), :] = part[slab(h, i), :]

        for h in range(2):
            far = col if h == 0 else last - col
            i = t - LAG * (last + far)
            live = (i >= 0) & (i < CHUNKS)

            @pl.when(live & (far > 0))
            def _():
                ag_copy(h, i).wait_recv()

            @pl.when(live & (far < last))
            def _():
                ag_copy(h, i).start()

            for s in range(sources):
                @pl.when(live & (chip == col * sources + s))
                def _():
                    xc[block(s, core, h, i), :] = xr[slab(h, i), :]

                spread(xc, x_sems, s, h, t - LAG * (last + far))

        for j in range(len(pairs) + 1):
            @pl.when(t == CHUNKS - 1 + LAG * j)
            def _():
                if j > 0:
                    g_copy(j - 1).wait_recv()
                    g_sum[j] = g_sum[j - 1] + g_in[j - 1]
                if j < len(pairs):
                    g_copy(j).start()

    xr_copy = pltpu.make_async_copy(xr, xr_out, out_sem.at[1])
    xr_copy.start()
    g_out[...] = g_sum[len(pairs)]

    @pl.loop(0, CHUNKS)
    def _(i):
        for s in range(sources):
            for h in range(2):
                sib_copy(xc, x_sems, s, h, i, 1 - core).wait_recv()

    xc_copy = pltpu.make_async_copy(xc, xc_out, out_sem.at[2])
    xc_copy.start()

    @pl.loop(0, CHUNKS)
    def _(i):
        for s in range(sources):
            for h in range(2):
                spread_sent(vc, v_sems, s, h, i)
                spread_sent(xc, x_sems, s, h, i)
        for h in range(2):
            depth = last - col if h == 0 else col

            @pl.when(depth < last)
            def _():
                rs_copy(h, i).wait_send()

            far = col if h == 0 else last - col

            @pl.when(far < last)
            def _():
                ag_copy(h, i).wait_send()

    for j in range(len(pairs)):
        g_copy(j).wait_send()
    vc_copy.wait()
    xr_copy.wait()
    xc_copy.wait()


def panel(matrix, vectors):
    m, n = matrix.shape
    nb = vectors.shape[1]
    rows, cols = lax.axis_size("row"), lax.axis_size("col")
    sources = rows // 2 // cols
    steps = (rows - 1).bit_length() + (cols - 1).bit_length()
    f32 = jnp.float32
    dma = pltpu.SemaphoreType.DMA
    whole = pl.BlockSpec(memory_space=pltpu.VMEM)
    hbm = pl.BlockSpec(memory_space=pl.ANY)
    return pl.pallas_call(
        functools.partial(panel_kernel, rows, cols),
        in_specs=[hbm, whole],
        out_specs=[hbm, hbm, hbm, whole],
        out_shape=[
            jax.ShapeDtypeStruct((n, nb), f32),
            jax.ShapeDtypeStruct((m, nb), f32),
            jax.ShapeDtypeStruct((n, nb), f32),
            jax.ShapeDtypeStruct((nb, nb), f32),
        ],
        scratch_shapes=[
            pltpu.VMEM((m, n), f32),
            pltpu.VMEM((n, nb), f32),
            pltpu.VMEM((n, 2 * nb), jnp.bfloat16),
            pltpu.VMEM((m, nb), f32),
            pltpu.VMEM((m, nb), f32),
            pltpu.VMEM((m, nb), f32),
            pltpu.VMEM((n, nb), f32),
            pltpu.VMEM((steps + 1, nb, nb), f32),
            pltpu.VMEM((steps, nb, nb), f32),
            dma((2, CHUNKS)),
            dma((3,)),
        ]
        + [dma((sources, 2, CHUNKS))] * 8
        + [dma((2, CHUNKS))] * 4
        + [dma((steps,))] * 2,
        compiler_params=pltpu.CompilerParams(
            collective_id=0, has_side_effects=True, vmem_limit_bytes=60 << 20
        ),
        name="panel_products",
    )(matrix, vectors)


def update_kernel(a_ref, v_ref, xr_ref, t_ref, g_ref, vc_ref, xc_ref, out_ref, left):
    rows = a_ref.shape[0]
    tall = min(1024, rows)

    @pl.when(pl.program_id(0) == 0)
    def _():
        half = 0.5 * wide_dot(wide_dot(t_ref[...], g_ref[...], TN), t_ref[...], NN)
        vectors = v_ref[...]
        l_high, l_low = split(wide_dot(vectors, t_ref[...], NT))
        w_high, w_low = split(
            wide_dot(xr_ref[...], t_ref[...], NN) - wide_dot(vectors, half + half.T, NN)
        )
        left[...] = jnp.concatenate([l_high, w_high, l_high, w_high, l_low, w_low], axis=1)

    x_high, x_low = split(xc_ref[...])
    v_high, v_low = split(vc_ref[...])
    right = jnp.concatenate([x_high, v_high, x_low, v_low, x_high, v_high], axis=1)
    for at in range(0, rows, tall):
        change = lax.dot_general(
            left[at : at + tall, :], right, NT, preferred_element_type=jnp.float32
        )
        out_ref[at : at + tall, :] = a_ref[at : at + tall, :] - change


def tile_update(matrix, vectors, x_rows, tfactor, cross, vec_cols, x_cols):
    rows, columns = matrix.shape
    nb = vectors.shape[1]
    block = min(256, columns)
    panel_rows = pl.BlockSpec((rows, nb), lambda i: (0, 0))
    small = pl.BlockSpec((nb, nb), lambda i: (0, 0))
    panel_cols = pl.BlockSpec((block, nb), lambda i: (i, 0))
    tile = pl.BlockSpec((rows, block), lambda i: (0, i))
    return pl.pallas_call(
        update_kernel,
        grid=(columns // block,),
        in_specs=[tile, panel_rows, panel_rows, small, small, panel_cols, panel_cols],
        out_specs=tile,
        out_shape=jax.ShapeDtypeStruct((rows, columns), jnp.float32),
        scratch_shapes=[pltpu.VMEM((rows, 6 * nb), jnp.bfloat16)],
        compiler_params=pltpu.CompilerParams(vmem_limit_bytes=56 << 20),
        name="tile_update",
    )(matrix, vectors, x_rows, tfactor, cross, vec_cols, x_cols)


def shards(matrix, vectors, tfactor):
    vec_cols, x_rows, x_cols, cross = panel(matrix, vectors)
    return tile_update(matrix, vectors, x_rows, tfactor, cross, vec_cols, x_cols)


def solution(mesh):
    in_specs = (P("row", "col"), P("row", None), P())
    out_specs = P("row", "col")
    return jax.shard_map(shards, mesh=mesh, in_specs=in_specs, out_specs=out_specs, check_vma=False)
```

```python
import functools

import jax
import jax.numpy as jnp
from jax import lax
from jax.experimental import pallas as pl
from jax.experimental.pallas import tpu as pltpu
from jax.sharding import PartitionSpec as P

NN = (((1,), (0,)), ((), ()))
NT = (((1,), (1,)), ((), ()))
TN = (((0,), (0,)), ((), ()))


def split(values):
    high = values.astype(jnp.bfloat16)
    low = (values - high.astype(jnp.float32)).astype(jnp.bfloat16)
    return high, low


def wide_dot(left, right, dims):
    l_high, l_low = split(left)
    r_high, r_low = split(right)
    return (
        lax.dot_general(l_high, r_high, dims, preferred_element_type=jnp.float32)
        + lax.dot_general(l_high, r_low, dims, preferred_element_type=jnp.float32)
        + lax.dot_general(l_low, r_high, dims, preferred_element_type=jnp.float32)
    )


CHUNKS = 8
LAG = 3
MESH = pl.DeviceIdType.MESH


def remote(src, dst, send_sem, recv_sem, device):
    return pltpu.make_async_remote_copy(
        src_ref=src, dst_ref=dst, send_sem=send_sem, recv_sem=recv_sem,
        device_id=device, device_id_type=MESH,
    )


def panel_kernel(
    row_count, col_count, a_hbm, v_ref, vc_out, xr_out, xc_out, g_out,
    a, vc, v2, part, rs_in, xr, xc, g_sum, g_in,
    a_sem, out_sem, v_ring_s, v_ring_r, v_sib_s, v_sib_r, x_ring_s, x_ring_r, x_sib_s, x_sib_r,
    rs_s, rs_r, ag_s, ag_r, g_s, g_r,
):
    m, nb = v_ref.shape
    half = m // 2
    chunk = half // CHUNKS
    chips = row_count // 2
    sources = chips // col_count
    last = col_count - 1
    wide = 1
    while wide * wide < chips:
        wide *= 2

    row, col = lax.axis_index("row"), lax.axis_index("col")
    chip, core = row // 2, row % 2

    def snake(at):
        y, x = at // wide, at % wide
        return y * wide + x + (y % 2) * (wide - 1 - 2 * x)

    place = snake(chip)
    sibling = (row + 1 - 2 * core, col)
    onward = (snake((place + 1) % chips) * 2 + core, col)
    backward = (snake((place + chips - 1) % chips) * 2 + core, col)
    ring = (onward, backward)
    right, left = (row, (col + 1) % col_count), (row, (col + last) % col_count)
    pairs = []
    bit = 1
    while bit < row_count:
        pairs.append((row + (1 - 2 * ((row // bit) % 2)) * bit, col))
        bit *= 2
    bit = 1
    while bit < col_count:
        pairs.append((row, col + (1 - 2 * ((col // bit) % 2)) * bit))
        bit *= 2

    def slab(h, i):
        return pl.ds(pl.multiple_of(h * half + i * chunk, chunk), chunk)

    def load(h, i):
        return pltpu.make_async_copy(a_hbm.at[slab(h, i)], a.at[slab(h, i)], a_sem.at[h, i])

    @pl.loop(0, CHUNKS)
    def _(i):
        load(0, i).start()
        load(1, i).start()

    barrier = pltpu.get_barrier_semaphore()
    greeted = [sibling, onward, backward, right, left] + pairs
    for device in greeted:
        pl.semaphore_signal(barrier, inc=1, device_id=device, device_id_type=MESH)
    pl.semaphore_wait(barrier, len(greeted))

    def distances(s):
        start = snake(col * sources + s)
        return (place - start + chips) % chips, (start - place + chips) % chips

    def block(s, whose, h, i):
        return pl.ds(pl.multiple_of((2 * s + whose) * m + h * half + i * chunk, chunk), chunk)

    def ring_copy(buf, sems, s, h, i):
        at = buf.at[block(s, core, h, i)]
        return remote(at, at, sems[0].at[s, h, i], sems[1].at[s, h, i], ring[h])

    def sib_copy(buf, sems, s, h, i, whose):
        at = buf.at[block(s, whose, h, i)]
        return remote(at, at, sems[2].at[s, h, i], sems[3].at[s, h, i], sibling)

    def spread(buf, sems, s, h, step):
        away = distances(s)[h]
        i = step - LAG * away
        live = (i >= 0) & (i < CHUNKS)

        @pl.when(live & (away > 0))
        def _():
            ring_copy(buf, sems, s, h, i).wait_recv()

        @pl.when(live & (away < chips - 1))
        def _():
            ring_copy(buf, sems, s, h, i).start()

        @pl.when(live)
        def _():
            sib_copy(buf, sems, s, h, i, core).start()

    def spread_sent(buf, sems, s, h, i):
        @pl.when(distances(s)[h] < chips - 1)
        def _():
            ring_copy(buf, sems, s, h, i).wait_send()

        sib_copy(buf, sems, s, h, i, core).wait_send()

    v_sems = (v_ring_s, v_ring_r, v_sib_s, v_sib_r)
    x_sems = (x_ring_s, x_ring_r, x_sib_s, x_sib_r)

    for s in range(sources):
        @pl.when(chip == col * sources + s)
        def _():
            vc[pl.ds(pl.multiple_of((2 * s + core) * m, m), m), :] = v_ref[...]

    @pl.loop(0, CHUNKS + LAG * (chips - 1))
    def _(t):
        for s in range(sources):
            for h in range(2):
                spread(vc, v_sems, s, h, t)

    @pl.loop(0, CHUNKS)
    def _(i):
        for s in range(sources):
            for h in range(2):
                sib_copy(vc, v_sems, s, h, i, 1 - core).wait_recv()

    vc_copy = pltpu.make_async_copy(vc, vc_out, out_sem.at[0])
    vc_copy.start()

    v_high, v_low = split(vc[...])
    v2[:, :nb] = v_high
    v2[:, nb:] = v_low
    g_sum[0] = jnp.zeros((nb, nb), jnp.float32)

    def rs_copy(h, i):
        return remote(
            part.at[slab(h, i)], rs_in.at[slab(h, i)], rs_s.at[h, i], rs_r.at[h, i], (left, right)[h]
        )

    def ag_copy(h, i):
        at = xr.at[slab(h, i)]
        return remote(at, at, ag_s.at[h, i], ag_r.at[h, i], (right, left)[h])

    def g_copy(j):
        return remote(g_sum.at[j], g_in.at[j], g_s.at[j], g_r.at[j], pairs[j])

    @pl.loop(0, CHUNKS + LAG * (2 * last + chips - 1))
    def _(t):
        @pl.when(t < CHUNKS)
        def _():
            load(0, t).wait()
            load(1, t).wait()
            parts = split(a[slab(0, t), :]) + split(a[slab(1, t), :])
            both = jnp.dot(jnp.concatenate(parts, axis=0), v2[...], preferred_element_type=jnp.float32)
            both = both[:, :nb] + both[:, nb:]
            first = both[:chunk] + both[chunk : 2 * chunk]
            second = both[2 * chunk : 3 * chunk] + both[3 * chunk :]
            part[slab(0, t), :] = first
            part[slab(1, t), :] = second
            g_sum[0] += wide_dot(v_ref[slab(0, t), :], first, TN) + wide_dot(
                v_ref[slab(1, t), :], second, TN
            )

        for h in range(2):
            depth = last - col if h == 0 else col
            i = t - LAG * depth
            live = (i >= 0) & (i < CHUNKS)

            @pl.when(live & (depth > 0))
            def _():
                rs_copy(h, i).wait_recv()
                part[slab(h, i), :] += rs_in[slab(h, i), :]

            @pl.when(live & (depth < last))
            def _():
                rs_copy(h, i).start()

            @pl.when(live & (depth == last))
            def _():
                xr[slab(h, i), :] = part[slab(h, i), :]

        for h in range(2):
            far = col if h == 0 else last - col
            i = t - LAG * (last + far)
            live = (i >= 0) & (i < CHUNKS)

            @pl.when(live & (far > 0))
            def _():
                ag_copy(h, i).wait_recv()

            @pl.when(live & (far < last))
            def _():
                ag_copy(h, i).start()

            for s in range(sources):
                @pl.when(live & (chip == col * sources + s))
                def _():
                    xc[block(s, core, h, i), :] = xr[slab(h, i), :]

                spread(xc, x_sems, s, h, t - LAG * (last + far))

        for j in range(len(pairs) + 1):
            @pl.when(t == CHUNKS - 1 + LAG * j)
            def _():
                if j > 0:
                    g_copy(j - 1).wait_recv()
                    g_sum[j] = g_sum[j - 1] + g_in[j - 1]
                if j < len(pairs):
                    g_copy(j).start()

    xr_copy = pltpu.make_async_copy(xr, xr_out, out_sem.at[1])
    xr_copy.start()
    g_out[...] = g_sum[len(pairs)]

    @pl.loop(0, CHUNKS)
    def _(i):
        for s in range(sources):
            for h in range(2):
                sib_copy(xc, x_sems, s, h, i, 1 - core).wait_recv()

    xc_copy = pltpu.make_async_copy(xc, xc_out, out_sem.at[2])
    xc_copy.start()

    @pl.loop(0, CHUNKS)
    def _(i):
        for s in range(sources):
            for h in range(2):
                spread_sent(vc, v_sems, s, h, i)
                spread_sent(xc, x_sems, s, h, i)
        for h in range(2):
            depth = last - col if h == 0 else col

            @pl.when(depth < last)
            def _():
                rs_copy(h, i).wait_send()

            far = col if h == 0 else last - col

            @pl.when(far < last)
            def _():
                ag_copy(h, i).wait_send()

    for j in range(len(pairs)):
        g_copy(j).wait_send()
    vc_copy.wait()
    xr_copy.wait()
    xc_copy.wait()


def panel(matrix, vectors):
    m, n = matrix.shape
    nb = vectors.shape[1]
    rows, cols = lax.axis_size("row"), lax.axis_size("col")
    sources = rows // 2 // cols
    steps = (rows - 1).bit_length() + (cols - 1).bit_length()
    f32 = jnp.float32
    dma = pltpu.SemaphoreType.DMA
    whole = pl.BlockSpec(memory_space=pltpu.VMEM)
    hbm = pl.BlockSpec(memory_space=pl.ANY)
    return pl.pallas_call(
        functools.partial(panel_kernel, rows, cols),
        in_specs=[hbm, whole],
        out_specs=[hbm, hbm, hbm, whole],
        out_shape=[
            jax.ShapeDtypeStruct((n, nb), f32),
            jax.ShapeDtypeStruct((m, nb), f32),
            jax.ShapeDtypeStruct((n, nb), f32),
            jax.ShapeDtypeStruct((nb, nb), f32),
        ],
        scratch_shapes=[
            pltpu.VMEM((m, n), f32),
            pltpu.VMEM((n, nb), f32),
            pltpu.VMEM((n, 2 * nb), jnp.bfloat16),
            pltpu.VMEM((m, nb), f32),
            pltpu.VMEM((m, nb), f32),
            pltpu.VMEM((m, nb), f32),
            pltpu.VMEM((n, nb), f32),
            pltpu.VMEM((steps + 1, nb, nb), f32),
            pltpu.VMEM((steps, nb, nb), f32),
            dma((2, CHUNKS)),
            dma((3,)),
        ]
        + [dma((sources, 2, CHUNKS))] * 8
        + [dma((2, CHUNKS))] * 4
        + [dma((steps,))] * 2,
        compiler_params=pltpu.CompilerParams(
            collective_id=0, has_side_effects=True, vmem_limit_bytes=60 << 20
        ),
        name="panel_products",
    )(matrix, vectors)


def update_kernel(a_ref, v_ref, xr_ref, t_ref, g_ref, vc_ref, xc_ref, out_ref, right, middle):
    nb = v_ref.shape[1]
    columns = a_ref.shape[1]
    wide = min(512, columns)

    @pl.when(pl.program_id(0) == 0)
    def _():
        half = 0.5 * wide_dot(wide_dot(t_ref[...], g_ref[...], TN), t_ref[...], NN)
        middle[...] = half + half.T
        for at, ref in ((0, xc_ref), (nb, vc_ref)):
            high, low = split(ref[...])
            right[:, at : at + nb] = high
            right[:, 2 * nb + at : 3 * nb + at] = low
            right[:, 4 * nb + at : 5 * nb + at] = high

    vectors = v_ref[...]
    l_high, l_low = split(wide_dot(vectors, t_ref[...], NT))
    w_high, w_low = split(
        wide_dot(xr_ref[...], t_ref[...], NN) - wide_dot(vectors, middle[...], NN)
    )
    left = jnp.concatenate([l_high, w_high, l_high, w_high, l_low, w_low], axis=1)
    for at in range(0, columns, wide):
        change = lax.dot_general(
            left, right[at : at + wide, :], NT, preferred_element_type=jnp.float32
        )
        out_ref[:, at : at + wide] = a_ref[:, at : at + wide] - change


def tile_update(matrix, vectors, x_rows, tfactor, cross, vec_cols, x_cols):
    rows, columns = matrix.shape
    nb = vectors.shape[1]
    block = min(256, rows)
    panel_rows = pl.BlockSpec((block, nb), lambda i: (i, 0))
    small = pl.BlockSpec((nb, nb), lambda i: (0, 0))
    panel_cols = pl.BlockSpec((columns, nb), lambda i: (0, 0))
    tile = pl.BlockSpec((block, columns), lambda i: (i, 0))
    return pl.pallas_call(
        update_kernel,
        grid=(rows // block,),
        in_specs=[tile, panel_rows, panel_rows, small, small, panel_cols, panel_cols],
        out_specs=tile,
        out_shape=jax.ShapeDtypeStruct((rows, columns), jnp.float32),
        scratch_shapes=[
            pltpu.VMEM((columns, 6 * nb), jnp.bfloat16),
            pltpu.VMEM((nb, nb), jnp.float32),
        ],
        compiler_params=pltpu.CompilerParams(vmem_limit_bytes=56 << 20),
        name="tile_update",
    )(matrix, vectors, x_rows, tfactor, cross, vec_cols, x_cols)


def shards(matrix, vectors, tfactor):
    vec_cols, x_rows, x_cols, cross = panel(matrix, vectors)
    return tile_update(matrix, vectors, x_rows, tfactor, cross, vec_cols, x_cols)


def solution(mesh):
    in_specs = (P("row", "col"), P("row", None), P())
    out_specs = P("row", "col")
    return jax.shard_map(shards, mesh=mesh, in_specs=in_specs, out_specs=out_specs, check_vma=False)
```
